128 devices in a mesh: tile: 32 (over x, y, core), lev: 4 (over z).
Axes of the slice: x: 4, y: 4, z: 4, core: 2. Of those that a mesh axis runs over, the one named last changes fastest.
Arguments:
- state: float32 [32, 80, 16384], P('lev', None, 'tile'), may hold values from -6 to 6
- obs_prior: float32 [8, 80, 2048], P(None, None, ('tile', 'lev')), may hold values from -6 to 6
- obs_value: float32 [8, 2048], P(None, ('tile', 'lev')), may hold values from -8 to 8
- obs_error: float32 [8, 2048], P(None, ('tile', 'lev')), may hold values from 0.3 to 3
- obs_place: float32 [8, 2048], P(None, ('tile', 'lev')), may hold values from 0 to 1
- obs_height: float32 [8, 2048], P(None, ('tile', 'lev')), may hold values from 0 to 32
- tile_blocks: int32 [8, 32, 6], P(None, 'tile'), may hold values from 0 to 15, as said below
- tile_counts: int32 [8, 32], P(None, 'tile'), may hold values from 1 to 6, as said below
- loc_blocks: bfloat16 [8, 768, 16384], P(None, None, 'tile'), may hold values from 0.19921875 to 1
- pair_mask: int32 [8, 16, 8, 16], replicated, may hold values 0 or 1
Outputs:
- analysis: float32 [32, 80, 16384], P('lev', None, 'tile')
- obs_post: float32 [8, 80, 2048], P(None, None, ('tile', 'lev'))
The draws below stay inside these ranges and needn't reach their ends.
Inputs may be any that keep to these rules, and one draw needn't show every extreme that they name: `tile_blocks`: each row lists 6 different blocks. `tile_counts`: in every batch some tile uses all 6 of its blocks.
All inputs are finite; a program needn't handle non-finite values.
Results may differ from the reference program's by a relative error of at most 0.035.
Values may be sent and summed in bfloat16 or wider, within the bound.
A program may use at most 128 MiB of HBM per device.

```python
import math
import jax
import jax.numpy as jnp
from jax import lax

K = 80
NB = 8
B = 2048
OBLK = 128
MAXB = 6
COL_DEV = 512
NOB = 16
NTILES = 32
LEV = 32
COLS = 16384


def draw_tile_blocks(key, part):
    key = jax.random.fold_in(key, 11)
    key_list = jax.random.split(key, NB * NTILES)
    picked = jax.vmap(lambda single: jax.random.permutation(single, NOB)[:MAXB])(key_list)
    return picked.reshape(NB, NTILES, MAXB).astype(jnp.int32)


def draw_tile_counts(key, part):
    key = jax.random.fold_in(key, 23)
    first_key, second_key, third_key = jax.random.split(key, 3)
    first_draw = jax.random.randint(first_key, (NB, NTILES), 1, MAXB + 1)
    second_draw = jax.random.randint(second_key, (NB, NTILES), 1, MAXB + 1)
    counts = jnp.minimum(first_draw, second_draw)
    full_tile = jax.random.randint(third_key, (NB, 1), 0, NTILES)
    counts = jnp.where(jnp.arange(NTILES)[None, :] == full_tile, MAXB, counts)
    return counts.astype(jnp.int32)


def touch_ends(values, own_key, smallest, high):
    spot = [jax.random.randint(jax.random.fold_in(own_key, axis), (), 0, length) for axis, length in enumerate(values.shape)]
    longest = values.shape.index(max(values.shape))
    beside = spot[:longest] + [(spot[longest] + 1) % values.shape[longest]] + spot[longest + 1:]
    return values.at[tuple(spot)].set(smallest).at[tuple(beside)].set(high)


def shard_levels(key, extent, pieces, least, high):
    loudness = 1.0
    for axis_at, parts in pieces:
        draws = jax.random.uniform(jax.random.fold_in(jax.random.fold_in(key, 6), axis_at), (parts,), jnp.float32, least / len(pieces), high / len(pieces))
        loudness = loudness * jnp.repeat(jnp.exp(draws), extent[axis_at] // parts).reshape((-1,) + (1,) * (len(extent) - 1 - axis_at))
    return loudness


def gaussian(own_key, shape, width, most, cuts=(), kind=jnp.bfloat16):
    values = width * jax.random.normal(own_key, shape, jnp.float32)
    if cuts:
        values = values * shard_levels(own_key, shape, cuts, -0.22, 0.18)
    return jnp.clip(values, -most, most).astype(kind)


def setup_inputs(seed: int = 0) -> dict:
    seeds = jax.random.split(jax.random.key(seed), 11)
    return {
        "state": gaussian(seeds[0], (LEV, K, COLS), 1.0, 6.0, ((0, 4), (2, 32)), jnp.float32),
        "obs_prior": gaussian(seeds[1], (NB, K, B), 1.0, 6.0, ((2, 128),), jnp.float32),
        "obs_value": gaussian(seeds[2], (NB, B), 1.5, 8.0, ((1, 128),), jnp.float32),
        "obs_error": jnp.clip(jnp.exp(math.log(3.0) - 2.3025851 * jax.random.uniform(seeds[3], (NB, B), jnp.float32) ** shard_levels(seeds[3], (NB, B), ((1, 128),), -0.2, 0.2)), 0.3, 3.0),
        "obs_place": jnp.clip(1.0 * jax.random.uniform(seeds[4], (NB, B), jnp.float32) ** shard_levels(seeds[4], (NB, B), ((1, 128),), -0.2, 0.2), 0.0, 1.0),
        "obs_height": jnp.clip(32.0 * jax.random.uniform(seeds[5], (NB, B), jnp.float32) ** shard_levels(seeds[5], (NB, B), ((1, 128),), -0.2, 0.2), 0.0, 32.0),
        "tile_blocks": draw_tile_blocks(jax.random.fold_in(seeds[10], 71), 0),
        "tile_counts": draw_tile_counts(jax.random.fold_in(seeds[10], 71), 0),
        "loc_blocks": jnp.clip(0.19921875 + 0.80078125 * jax.random.uniform(seeds[8], (NB, MAXB * OBLK, COLS), jnp.float32) ** shard_levels(seeds[8], (NB, MAXB * OBLK, COLS), ((2, 32),), -0.2, 0.2), 0.19921875, 1.0).astype(jnp.bfloat16),
        "pair_mask": touch_ends((jax.random.randint(seeds[9], (NB, NOB, NB, NOB), 0, 2) < 1).astype(jnp.int32), jax.random.fold_in(seeds[9], 1), 0, 1),
    }


EPS = 1e-05
REACH = 0.25

def closeness(gap, reach):
    return 1.0 / (1.0 + (gap / reach) ** 2)

def pick_blocks(values, block_ids):
    shaped = values.reshape(values.shape[:-1] + (NOB, OBLK))
    chosen = jnp.take(shaped, block_ids, axis=values.ndim - 1)
    return chosen.reshape(values.shape[:-1] + (MAXB * OBLK,))

def tile_update(column_block, block_ids, used_count, locality, anomaly_low, delta_low, variance, height_row, level_pos, vreach):
    chosen_anom = pick_blocks(anomaly_low, block_ids)
    chosen_delta = pick_blocks(delta_low, block_ids)
    chosen_var = pick_blocks(variance, block_ids)
    chosen_height = pick_blocks(height_row, block_ids)
    valid = jnp.repeat((jnp.arange(MAXB) < used_count).astype(jnp.float32), OBLK)
    average = lax.optimization_barrier(jnp.mean(column_block, axis=1, keepdims=True))
    state_low = (column_block - average).astype(jnp.bfloat16)
    covar = jnp.einsum('km,lkc->lmc', chosen_anom.astype(jnp.float32), state_low.astype(jnp.float32)) / (K - 1)
    vertical = closeness(level_pos[:, None] - chosen_height[None, :], vreach)
    scaling = vertical * (valid * (4.0 / math.sqrt(MAXB * OBLK)) / chosen_var)[None, :]
    gain_low = (covar * scaling[:, :, None] * locality.astype(jnp.float32)[None]).astype(jnp.bfloat16)
    return column_block + jnp.einsum('km,lmc->lkc', chosen_delta.astype(jnp.float32), gain_low.astype(jnp.float32))

def reference(state, obs_prior, obs_value, obs_error, obs_place, obs_height, tile_blocks, tile_counts, loc_blocks, pair_mask):
    prior_list = [obs_prior[batch_id] for batch_id in range(NB)]
    analysis = state
    level_pos = jnp.arange(LEV, dtype=jnp.float32) + 0.5
    vreach = LEV / 4.0
    couple = 4.0 / math.sqrt(B)
    for batch_id in range(NB):
        current = prior_list[batch_id]
        average = lax.optimization_barrier(jnp.mean(current, axis=0))
        anomaly = current - average
        variance = lax.optimization_barrier(jnp.sum(anomaly * anomaly, axis=0)) / (K - 1) + EPS
        mismatch = obs_value[batch_id] - average
        obs_err = obs_error[batch_id]
        gamma_sq = jnp.sum(mismatch * mismatch) / jnp.sum(variance + obs_err)
        inflated = gamma_sq * variance
        increment = inflated / (inflated + obs_err) * mismatch
        factor = jnp.sqrt(gamma_sq * obs_err / (inflated + obs_err)) - 1.0
        anomaly_low = anomaly.astype(jnp.bfloat16)
        delta_low = (increment + factor * anomaly_low.astype(jnp.float32)).astype(jnp.bfloat16)
        prior_list[batch_id] = current + delta_low.astype(jnp.float32)
        for later_id in range(batch_id + 1, NB):
            other_obs = prior_list[later_id]
            other_low = (other_obs - lax.optimization_barrier(jnp.mean(other_obs, axis=0))).astype(jnp.bfloat16)
            covar = lax.dot_general(other_low, anomaly_low, (((0,), (0,)), ((), ())), preferred_element_type=jnp.float32) / (K - 1)
            block_mask = jnp.repeat(jnp.repeat(pair_mask[later_id, :, batch_id, :], OBLK, axis=0), OBLK, axis=1).astype(jnp.float32)
            locality = block_mask * closeness(obs_place[later_id][:, None] - obs_place[batch_id][None, :], REACH)
            gain_low = (covar * locality * couple / variance[None, :]).astype(jnp.bfloat16)
            prior_list[later_id] = other_obs + lax.dot_general(delta_low, gain_low, (((1,), (1,)), ((), ())), preferred_element_type=jnp.float32)
        tile_view = jnp.moveaxis(analysis.reshape(LEV, K, NTILES, COL_DEV), 2, 0)
        loc_view = jnp.moveaxis(loc_blocks[batch_id].reshape(MAXB * OBLK, NTILES, COL_DEV), 1, 0)

        def one_tile(packed):
            return tile_update(packed[0], packed[1], packed[2], packed[3], anomaly_low, delta_low, variance, obs_height[batch_id], level_pos, vreach)
        new_tiles = lax.map(one_tile, (tile_view, tile_blocks[batch_id], tile_counts[batch_id], loc_view))
        analysis = jnp.moveaxis(new_tiles, 0, 2).reshape(LEV, K, COLS)
    return (analysis, jnp.stack(prior_list))
```

```python
import math

import jax
import jax.numpy as jnp
from jax import lax
from jax.experimental import pallas as pl
from jax.experimental.pallas import tpu as pltpu
from jax.sharding import PartitionSpec as P

MESH = pl.DeviceIdType.MESH
F32 = jnp.float32
BF16 = jnp.bfloat16

K = 80
NB = 8
B = 2048
OBLK = 128
NOB = 16
MAXB = 6
LEVD = 8
COLD = 512
GRP = 8
OWN = OBLK // GRP

EPS = 1e-05
INV_REACH = 4.0
INV_VREACH = 0.125
COUPLE = 4.0 / math.sqrt(B) / (K - 1)
SCOUPLE = 4.0 / math.sqrt(MAXB * OBLK) / (K - 1)


def device(x, y, core, z):
    return ((x * 4 + y) * 2 + core, z)


def kernel(
    state_hbm,
    prior_ref,
    value_ref,
    error_ref,
    place_ref,
    height_ref,
    blocks_ref,
    counts_ref,
    loc_hbm,
    mask_hbm,
    x_ref,
    post_ref,
    piece,
    yo,
    aux,
    pcol,
    mrow,
    maskv,
    ab,
    st,
    abc,
    stc,
    rows,
    dyb,
    dys,
    near,
    rr,
    aet,
    abt,
    dch,
    scl,
    locv,
    state_sem,
    loc_sem,
    mask_sem,
    psend,
    precv,
    ssend,
    srecv,
    bsend,
    brecv,
):
    t = lax.axis_index("tile")
    z = lax.axis_index("lev")
    x, y, core = t // 8, (t // 2) % 4, t % 2
    own = x * 4 + y
    seat = core * 4 + z

    load_state = pltpu.make_async_copy(state_hbm, x_ref, state_sem)
    load_state.start()
    load_mask = pltpu.make_async_copy(mask_hbm.at[:, own], maskv, mask_sem)
    load_mask.start()

    def load_loc(c):
        return pltpu.make_async_copy(loc_hbm.at[c], locv.at[c], loc_sem.at[c])

    for c in range(NB):
        load_loc(c).start()

    column = []
    for step in range(1, GRP):
        other = lax.rem(seat + step, GRP)
        column.append(device(x, y, other // 4, lax.rem(other, 4)))
    plane = []
    for dx in range(4):
        for dy in range(4):
            if dx or dy:
                plane.append(device(lax.rem(x + dx, 4), lax.rem(y + dy, 4), core, z))

    barrier = pltpu.get_barrier_semaphore()
    for peer in column + plane:
        pl.semaphore_signal(barrier, inc=1, device_id=peer, device_id_type=MESH)

    pad = jnp.zeros((16, 128 - 5 * OWN), F32)
    for e in range(NB):
        parts = [prior_ref[e, 16 * g : 16 * (g + 1), :] for g in range(5)]
        piece[seat, 1 + e] = jnp.concatenate(parts + [pad], axis=1)
    packed = jnp.concatenate(
        [value_ref[...], error_ref[...], place_ref[...] * INV_REACH, height_ref[...], jnp.zeros((NB, 64), F32)], axis=1
    )
    piece[seat, 0] = jnp.concatenate([packed, jnp.zeros((8, 128), F32)], axis=0)

    pl.semaphore_wait(barrier, len(column) + len(plane))

    def spread_pieces(part, first, count):
        for peer in column:
            ref = piece.at[seat, pl.ds(first, count)]
            pltpu.make_async_remote_copy(
                src_ref=ref,
                dst_ref=ref,
                send_sem=psend.at[part],
                recv_sem=precv.at[part],
                device_id=peer,
                device_id_type=MESH,
            ).start()

    def take_pieces(part, first, count, sem):
        ref = piece.at[pl.ds(0, GRP - 1), pl.ds(first, count)]
        pltpu.make_async_copy(ref, ref, sem.at[part]).wait()

    spread_pieces(0, 0, 2)
    spread_pieces(1, 2, NB - 1)

    load_mask.wait()
    eye = lax.broadcasted_iota(jnp.int32, (NOB, NOB), 0) == lax.broadcasted_iota(jnp.int32, (NOB, NOB), 1)
    for e in range(1, NB):
        for c in range(e):
            chosen = jnp.where(eye, maskv[e, c : c + 1, :].astype(F32), 0.0)
            mrow[e, c] = jnp.broadcast_to(jnp.sum(chosen, axis=1, keepdims=True), (NOB, 128))

    group = lax.broadcasted_iota(jnp.int32, (16, 128), 1) // OWN

    def gathered(slab, g):
        total = jnp.zeros((16, 128), F32)
        for s in range(GRP):
            moved = pltpu.roll(piece[s, slab], ((s - g) * OWN) % 128, 1)
            total = jnp.where(group == s, moved, total)
        return total

    def unpack(e):
        for g in range(5):
            yo[e, pl.ds(16 * g, 16), :] = gathered(1 + e, g)

    take_pieces(0, 0, 2, precv)
    for g in range(4):
        aux[g] = gathered(0, g)[0:NB]
    unpack(0)

    def copies(e, ref, send, recv):
        mine = ref.at[e, own]
        for peer in plane:
            pltpu.make_async_remote_copy(
                src_ref=mine,
                dst_ref=mine,
                send_sem=send.at[e],
                recv_sem=recv.at[e],
                device_id=peer,
                device_id_type=MESH,
            ).start()

    def publish(e):
        now = yo[e]
        average = jnp.sum(now, axis=0, keepdims=True) * (1.0 / K)
        anomaly = now - average
        variance = jnp.sum(anomaly * anomaly, axis=0, keepdims=True) * (1.0 / (K - 1)) + EPS
        here = pl.ds(e, 1)
        st[e, own] = jnp.concatenate(
            [
                variance,
                aux[0, here, :] - average,
                aux[1, here, :],
                aux[2, here, :],
                aux[3, here, :],
                jnp.zeros((3, 128), F32),
            ],
            axis=0,
        )
        copies(e, st, ssend, srecv)
        ab[e, own] = anomaly.astype(BF16)
        copies(e, ab, bsend, brecv)

    def take(e, ref, sem):
        some = ref.at[e, pl.ds(0, NOB - 1)]
        pltpu.make_async_copy(some, some, sem.at[e]).wait()

    publish(0)
    take_pieces(1, 2, NB - 1, precv)
    pl.loop(1, NB)(unpack)

    @pl.loop(0, NB)
    def _(e):
        pcol[e] = jnp.transpose(jnp.broadcast_to(aux[2, pl.ds(e, 1), :], (128, 128)))

    def nearness(c, e):
        mine = pcol[e]
        for b in range(NOB):
            cut = slice(b * 128, (b + 1) * 128)
            gap = mine - st[c, b, 3:4, :]
            near[:, cut] = (mrow[e, c, b : b + 1, :] * pl.reciprocal(1.0 + gap * gap, approx=True)).astype(BF16)

    def transposed(e):
        now = yo[e]
        average = jnp.sum(now, axis=0, keepdims=True) * (1.0 / K)
        aet[...] = jnp.transpose(now - average).astype(BF16)

    def regress(c, e):
        for part in range(4):
            cut = slice(part * 512, (part + 1) * 512)
            theirs = jnp.concatenate([ab[c, part * 4 + i] for i in range(4)], axis=1)
            covar = jnp.dot(aet[...], theirs, preferred_element_type=F32)
            rr[:, cut] = covar.astype(BF16) * near[:, cut]
        yo[e] += lax.dot_general(dys[...], rr[...], (((1,), (1,)), ((), ())), preferred_element_type=F32)

    level = (lax.broadcasted_iota(jnp.int32, (LEVD, 128), 0) + z * LEVD).astype(F32) + 0.5

    load_state.wait()

    @pl.loop(0, NB)
    def _(c):
        @pl.when(c < NB - 1)
        def _():
            transposed(c + 1)

        take(c, st, srecv)
        variance, miss, error = st[c, :, 0, :], st[c, :, 1, :], st[c, :, 2, :]
        gamma = jnp.sum(miss * miss, keepdims=True) / jnp.sum(variance + error, keepdims=True)
        inflated = gamma * variance
        both = inflated + error
        rows[0] = inflated / both * miss
        rows[1] = jnp.sqrt(gamma * error / both) - 1.0
        rows[2] = COUPLE / variance

        @pl.when(c < NB - 1)
        def _():
            nearness(c, c + 1)

        take(c, ab, brecv)
        for b in range(NOB):
            low = (rows[0, b : b + 1, :] + rows[1, b : b + 1, :] * ab[c, b].astype(F32)).astype(BF16)
            dyb[b] = low
            dys[:, b * 128 : (b + 1) * 128] = (low.astype(F32) * rows[2, b : b + 1, :]).astype(BF16)

        @pl.when(c < NB - 1)
        def _():
            regress(c, c + 1)
            publish(c + 1)

        yo[c] += dyb[own].astype(F32)

        @pl.loop(c + 2, NB)
        def _(e):
            transposed(e)
            nearness(c, e)
            regress(c, e)

        abc[...] = ab[c]
        stc[...] = st[c]
        load_loc(c).wait()
        used = counts_ref[c, 0]
        for i in range(MAXB):
            block = blocks_ref[c, 0, i]
            cut = slice(i * 128, (i + 1) * 128)
            abt[cut, :] = jnp.transpose(abc[block].astype(F32)).astype(BF16)
            dch[:, cut] = dyb[block]
            theirs = stc[block]
            gap = (level - theirs[4:5, :]) * INV_VREACH
            weight = jnp.where(i < used, SCOUPLE, 0.0) / theirs[0:1, :]
            scl[:, i, :] = weight / (1.0 + gap * gap)

        def one_level(l):
            block = x_ref[l]
            low = (block - jnp.sum(block, axis=0, keepdims=True) * (1.0 / K)).astype(BF16)
            covar = jnp.dot(abt[...], low, preferred_element_type=F32)
            gain = covar.astype(BF16) * locv[c]
            delta = jnp.concatenate(
                [
                    (dch[:, i * 128 : (i + 1) * 128].astype(F32) * scl[l, i : i + 1, :]).astype(BF16)
                    for i in range(MAXB)
                ],
                axis=1,
            )
            x_ref[l] = block + jnp.dot(delta, gain, preferred_element_type=F32)

        pl.loop(0, LEVD, unroll=2)(one_level)

    for e in range(NB):
        post_ref[e] = pltpu.roll(yo[e], lax.rem(128 - seat * OWN, 128), 1)[:, 0:OWN]

    take_pieces(0, 0, 2, psend)
    take_pieces(1, 2, NB - 1, psend)

    @pl.loop(0, NB)
    def _(c):
        take(c, st, ssend)
        take(c, ab, bsend)


def per_device(*args):
    vmem = pl.BlockSpec(memory_space=pltpu.VMEM)
    smem = pl.BlockSpec(memory_space=pltpu.SMEM)
    hbm = pl.BlockSpec(memory_space=pl.ANY)
    dma = pltpu.SemaphoreType.DMA
    return pl.pallas_call(
        kernel,
        out_shape=(
            jax.ShapeDtypeStruct((LEVD, K, COLD), F32),
            jax.ShapeDtypeStruct((NB, K, OWN), F32),
        ),
        in_specs=[hbm, vmem, vmem, vmem, vmem, vmem, smem, smem, hbm, hbm],
        out_specs=(vmem, vmem),
        scratch_shapes=[
            pltpu.VMEM((GRP, 1 + NB, 16, 128), F32),
            pltpu.VMEM((NB, K, 128), F32),
            pltpu.VMEM((4, NB, 128), F32),
            pltpu.VMEM((NB, 128, 128), F32),
            pltpu.VMEM((NB, NB, NOB, 128), F32),
            pltpu.VMEM((NB, NB, NOB), jnp.int32),
            pltpu.VMEM((NB, NOB, K, 128), BF16),
            pltpu.VMEM((NB, NOB, 8, 128), F32),
            pltpu.VMEM((NOB, K, 128), BF16),
            pltpu.VMEM((NOB, 8, 128), F32),
            pltpu.VMEM((3, NOB, 128), F32),
            pltpu.VMEM((NOB, K, 128), BF16),
            pltpu.VMEM((K, B), BF16),
            pltpu.VMEM((128, B), BF16),
            pltpu.VMEM((128, B), BF16),
            pltpu.VMEM((128, K), BF16),
            pltpu.VMEM((MAXB * 128, K), BF16),
            pltpu.VMEM((K, MAXB * 128), BF16),
            pltpu.VMEM((LEVD, 8, 128), F32),
            pltpu.VMEM((NB, MAXB * 128, COLD), BF16),
            dma(()),
            dma((NB,)),
            dma(()),
            dma((2,)),
            dma((2,)),
            dma((NB,)),
            dma((NB,)),
            dma((NB,)),
            dma((NB,)),
        ],
        compiler_params=pltpu.CompilerParams(
            collective_id=0, has_side_effects=True, vmem_limit_bytes=48 * 2**20
        ),
    )(*args)


def solution(mesh):
    placed = (
        P("lev", None, "tile"),
        P(None, None, ("tile", "lev")),
        P(None, ("tile", "lev")),
        P(None, ("tile", "lev")),
        P(None, ("tile", "lev")),
        P(None, ("tile", "lev")),
        P(None, "tile", None),
        P(None, "tile"),
        P(None, None, "tile"),
        P(),
    )
    return jax.shard_map(
        per_device,
        mesh=mesh,
        in_specs=placed,
        out_specs=(P("lev", None, "tile"), P(None, None, ("tile", "lev"))),
        check_vma=False,
    )
```

```python
import math

import jax
import jax.numpy as jnp
from jax import lax
from jax.experimental import pallas as pl
from jax.experimental.pallas import tpu as pltpu
from jax.sharding import PartitionSpec as P

MESH = pl.DeviceIdType.MESH
F32 = jnp.float32
BF16 = jnp.bfloat16

K = 80
NB = 8
B = 2048
OBLK = 128
NOB = 16
MAXB = 6
LEVD = 8
COLD = 512
QUAD = 4
GRP = 8
OWN = OBLK // GRP

EPS = 1e-05
INV_REACH = 4.0
INV_VREACH = 0.125
COUPLE = 4.0 / math.sqrt(B) / (K - 1)
SCOUPLE = 4.0 / math.sqrt(MAXB * OBLK) / (K - 1)


def device(x, y, core, z):
    return ((x * 4 + y) * 2 + core, z)


def kernel(
    state_hbm,
    prior_hbm,
    value_hbm,
    error_hbm,
    place_hbm,
    height_hbm,
    blocks_hbm,
    counts_hbm,
    loc_hbm,
    mask_hbm,
    x_ref,
    post_ref,
    prior,
    vectors,
    blocks_ref,
    counts_ref,
    piece,
    yo,
    yx,
    yt,
    aux,
    pcol,
    mrow,
    maskv,
    ab,
    st,
    hx,
    abc,
    vhc,
    rows,
    dyb,
    dys,
    near,
    rr,
    aet,
    abt,
    dch,
    scl,
    locv,
    in_sem,
    loc_sem,
    psend,
    precv,
    hsend,
    hrecv,
    ssend,
    srecv,
    bsend,
    brecv,
    ysend,
    yrecv,
):
    t = lax.axis_index("tile")
    z = lax.axis_index("lev")
    x, y, core = t // 8, (t // 2) % 4, t % 2
    own = x * 4 + y
    seat = core * 4 + z
    sibling = device(x, y, 1 - core, z)

    column = []
    for step in (4, 2, 6, 1, 3, 5, 7):
        other = lax.rem(seat + step, GRP)
        column.append(device(x, y, other // 4, lax.rem(other, 4)))
    hops = [(min(dx, 4 - dx) + min(dy, 4 - dy), dx, dy) for dx in range(4) for dy in range(4) if dx or dy]
    plane = []
    for _, dx, dy in sorted(hops, key=lambda hop: -hop[0]):
        plane.append(device(lax.rem(x + dx, 4), lax.rem(y + dy, 4), core, z))

    barrier = pltpu.get_barrier_semaphore()
    for peer in plane + column:
        pl.semaphore_signal(barrier, inc=1, device_id=peer, device_id_type=MESH)

    small = [
        pltpu.make_async_copy(src, dst, in_sem.at[i])
        for i, (src, dst) in enumerate(
            [
                (prior_hbm, prior),
                (value_hbm, vectors.at[0]),
                (error_hbm, vectors.at[1]),
                (place_hbm, vectors.at[2]),
                (height_hbm, vectors.at[3]),
                (mask_hbm.at[:, own], maskv),
                (blocks_hbm, blocks_ref),
                (counts_hbm, counts_ref),
                (state_hbm, x_ref),
            ]
        )
    ]
    for copy in small:
        copy.start()

    def load_loc(c):
        return pltpu.make_async_copy(loc_hbm.at[c], locv.at[c], loc_sem.at[c])

    for c in range(NB):
        load_loc(c).start()

    for copy in small[:5]:
        copy.wait()
    for e in range(NB):
        piece[seat, 1 + e] = jnp.concatenate([prior[e], jnp.zeros((OWN, 128 - K), F32)], axis=1)
    square = jnp.concatenate([vectors[g] for g in range(4)] + [jnp.zeros((128 - 4 * NB, OWN), F32)], axis=0)
    square = jnp.concatenate([square, jnp.zeros((128, 128 - OWN), F32)], axis=1)
    piece[seat, 0] = jnp.transpose(square)[0:OWN]

    pl.semaphore_wait(barrier, len(column) + len(plane))

    def send(ref, send_sem, recv_sem, peers):
        for peer in peers:
            pltpu.make_async_remote_copy(
                src_ref=ref,
                dst_ref=ref,
                send_sem=send_sem,
                recv_sem=recv_sem,
                device_id=peer,
                device_id_type=MESH,
            ).start()

    def settle(ref, sem):
        pltpu.make_async_copy(ref, ref, sem).wait()

    send(piece.at[seat, pl.ds(0, 2)], psend.at[0], precv.at[0], column)
    send(piece.at[seat, pl.ds(2, NB - 1)], psend.at[1], precv.at[1], column)
    early = piece.at[pl.ds(0, GRP - 1), pl.ds(0, 2)]
    late = piece.at[pl.ds(0, GRP - 1), pl.ds(2, NB - 1)]

    small[5].wait()
    eye = lax.broadcasted_iota(jnp.int32, (NOB, NOB), 0) == lax.broadcasted_iota(jnp.int32, (NOB, NOB), 1)
    for e in range(1, NB):
        for c in range(e):
            chosen = jnp.where(eye, maskv[e, c : c + 1, :].astype(F32), 0.0)
            mrow[e, c] = jnp.broadcast_to(jnp.sum(chosen, axis=1, keepdims=True), (NOB, 128))

    def unpack(e):
        yo[e] = jnp.transpose(piece[:, 1 + e].reshape(128, 128))[0:K]

    settle(early, precv.at[0])
    vector_rows = jnp.transpose(piece[:, 0].reshape(128, 128))
    for g in range(4):
        aux[g] = vector_rows[g * NB : (g + 1) * NB] * (INV_REACH if g == 2 else 1.0)
    unpack(0)
    for e in range(NB):
        for g in range(1, 4):
            hx[own, e, g - 1 : g, :] = aux[g, e : e + 1, :]
        hx[own, e, 3:4, :] = jnp.zeros((1, 128), F32)

    def publish(e):
        now = yo[e]
        average = jnp.sum(now, axis=0, keepdims=True) * (1.0 / K)
        anomaly = now - average
        variance = jnp.sum(anomaly * anomaly, axis=0, keepdims=True) * (1.0 / (K - 1)) + EPS
        st[e, own, 0:1, :] = variance
        st[e, own, 1:2, :] = aux[0, pl.ds(e, 1), :] - average
        send(st.at[e, own], ssend.at[e], srecv.at[e], plane)
        ab[e, own] = anomaly.astype(BF16)
        send(ab.at[e, own], bsend.at[e], brecv.at[e], plane)

    def take(e, ref, sem):
        settle(ref.at[e, pl.ds(0, NOB - 1)], sem.at[e])

    send(hx.at[own, 0], hsend.at[0], hrecv.at[0], plane)
    publish(0)
    send(hx.at[own, pl.ds(1, NB - 1)], hsend.at[1], hrecv.at[1], plane)
    hx_first = hx.at[pl.ds(0, NOB - 1), 0]
    hx_rest = hx.at[pl.ds(0, NOB - 1), pl.ds(1, NB - 1)]
    settle(late, precv.at[1])
    pl.loop(1, NB)(unpack)

    @pl.loop(0, NB)
    def _(e):
        pcol[e] = jnp.transpose(jnp.broadcast_to(aux[2, pl.ds(e, 1), :], (128, 128)))

    def nearness(c, e):
        mine = pcol[e]
        for b in range(NOB):
            cut = slice(b * 128, (b + 1) * 128)
            gap = mine - hx[b, c, 1:2, :]
            near[:, cut] = pl.reciprocal(1.0 + gap * gap, approx=True).astype(BF16)

    def transposed(e):
        now = yo[e]
        average = jnp.sum(now, axis=0, keepdims=True) * (1.0 / K)
        aet[...] = jnp.transpose(now - average).astype(BF16)

    def regress(c, e):
        for part in range(4):
            cut = slice(part * 512, (part + 1) * 512)
            theirs = jnp.concatenate(
                [ab[c, b] * mrow[e, c, b : b + 1, :].astype(BF16) for b in range(part * 4, part * 4 + 4)], axis=1
            )
            covar = jnp.dot(aet[...], theirs, preferred_element_type=F32)
            rr[:, cut] = covar.astype(BF16) * near[:, cut]
        yo[e] += lax.dot_general(dys[...], rr[...], (((1,), (1,)), ((), ())), preferred_element_type=F32)

    level = (lax.broadcasted_iota(jnp.int32, (LEVD, 128), 0) + z * LEVD).astype(F32) + 0.5

    for copy in small[6:]:
        copy.wait()
    settle(hx_first, hrecv.at[0])

    def hand_over(e):
        return pltpu.make_async_remote_copy(
            src_ref=yo.at[e],
            dst_ref=yx.at[e],
            send_sem=ysend.at[e],
            recv_sem=yrecv.at[e],
            device_id=sibling,
            device_id_type=MESH,
        )

    def one_level(unit):
        c, l = unit // LEVD, unit % LEVD
        block = x_ref[l]
        low = (block - jnp.sum(block, axis=0, keepdims=True) * (1.0 / K)).astype(BF16)
        covar = jnp.dot(abt[c], low, preferred_element_type=F32)
        gain = covar.astype(BF16) * locv[c]
        delta = jnp.concatenate(
            [
                (dch[c, :, i * 128 : (i + 1) * 128].astype(F32) * scl[c, l, i : i + 1, :]).astype(BF16)
                for i in range(MAXB)
            ],
            axis=1,
        )
        x_ref[l] = block + jnp.dot(delta, gain, preferred_element_type=F32)

    def state_quad(quad):
        for i in range(QUAD):
            one_level(quad * QUAD + i)

    @pl.loop(0, NB)
    def _(c):
        @pl.when(c == 1)
        def _():
            settle(hx_rest, hrecv.at[1])

        @pl.when((c >= 1) & (c < NB - 1))
        def _():
            @pl.when(core == (c + 1) % 2)
            def _():
                hand_over(c + 1).wait_send()

            @pl.when(core != (c + 1) % 2)
            def _():
                hand_over(c + 1).wait_recv()
                yo[c + 1] = yx[c + 1]

        @pl.when(c < NB - 1)
        def _():
            transposed(c + 1)
            nearness(c, c + 1)

        take(c, st, srecv)
        variance, miss, error = st[c, :, 0, :], st[c, :, 1, :], hx[:, c, 0, :]
        gamma = jnp.sum(miss * miss, keepdims=True) / jnp.sum(variance + error, keepdims=True)
        inflated = gamma * variance
        both = inflated + error
        rows[0] = inflated / both * miss
        rows[1] = jnp.sqrt(gamma * error / both) - 1.0
        rows[2] = COUPLE / variance

        take(c, ab, brecv)
        for b in range(NOB):
            low = (rows[0, b : b + 1, :] + rows[1, b : b + 1, :] * ab[c, b].astype(F32)).astype(BF16)
            dyb[b] = low
            dys[:, b * 128 : (b + 1) * 128] = (low.astype(F32) * rows[2, b : b + 1, :]).astype(BF16)

        @pl.when(c < NB - 1)
        def _():
            regress(c, c + 1)
            publish(c + 1)

        @pl.loop(c + 2 + (c + core) % 2, NB, step=2)
        def _(e):
            transposed(e)
            nearness(c, e)
            regress(c, e)

            @pl.when(e == c + 2)
            def _():
                hand_over(e).start()

        abc[...] = ab[c]
        vhc[:, 0, :] = variance
        vhc[:, 1, :] = hx[:, c, 2, :]
        load_loc(c).wait()
        used = counts_ref[0, c]
        for i in range(MAXB):
            block = blocks_ref[i, 0, c]
            cut = slice(i * 128, (i + 1) * 128)
            abt[c, cut, :] = jnp.transpose(abc[block].astype(F32)).astype(BF16)
            dch[c, :, cut] = dyb[block]
            theirs = vhc[block]
            gap = (level - theirs[1:2, :]) * INV_VREACH
            weight = jnp.where(i < used, SCOUPLE, 0.0) / theirs[0:1, :]
            scl[c, :, i, :] = weight / (1.0 + gap * gap)

        first = jnp.where(c == 0, 0, 2 * c - 1)
        last = jnp.where(c >= NB - 2, 2 * c + 2, 2 * c + 1)
        pl.loop(jnp.where(c == NB - 1, 2 * c, first), last)(state_quad)

        final = yo[c] + dyb[own].astype(F32)
        yt[...] = jnp.transpose(final)
        post_ref[c] = yt[pl.ds(pl.multiple_of(seat * OWN, OWN), OWN), :]

    settle(early, psend.at[0])
    settle(late, psend.at[1])
    settle(hx_first, hsend.at[0])
    settle(hx_rest, hsend.at[1])

    @pl.loop(0, NB)
    def _(c):
        take(c, st, ssend)
        take(c, ab, bsend)


def per_device(state, prior, value, error, place, height, blocks, counts, loc, mask):
    vmem = pl.BlockSpec(memory_space=pltpu.VMEM)
    hbm = pl.BlockSpec(memory_space=pltpu.HBM)
    dma = pltpu.SemaphoreType.DMA
    analysis, post = pl.pallas_call(
        kernel,
        out_shape=(
            jax.ShapeDtypeStruct((LEVD, K, COLD), F32),
            jax.ShapeDtypeStruct((NB, OWN, K), F32),
        ),
        in_specs=[hbm] * 10,
        out_specs=(vmem, vmem),
        scratch_shapes=[
            pltpu.VMEM((NB, OWN, K), F32),
            pltpu.VMEM((4, NB, OWN), F32),
            pltpu.SMEM((MAXB, 1, NB), jnp.int32),
            pltpu.SMEM((1, NB), jnp.int32),
            pltpu.VMEM((GRP, 1 + NB, OWN, 128), F32),
            pltpu.VMEM((NB, K, 128), F32),
            pltpu.VMEM((NB, K, 128), F32),
            pltpu.VMEM((128, K), F32),
            pltpu.VMEM((4, NB, 128), F32),
            pltpu.VMEM((NB, 128, 128), F32),
            pltpu.VMEM((NB, NB, NOB, 128), F32),
            pltpu.VMEM((NB, NB, NOB), jnp.int32),
            pltpu.VMEM((NB, NOB, K, 128), BF16),
            pltpu.VMEM((NB, NOB, 2, 128), F32),
            pltpu.VMEM((NOB, NB, 4, 128), F32),
            pltpu.VMEM((NOB, K, 128), BF16),
            pltpu.VMEM((NOB, 2, 128), F32),
            pltpu.VMEM((3, NOB, 128), F32),
            pltpu.VMEM((NOB, K, 128), BF16),
            pltpu.VMEM((K, B), BF16),
            pltpu.VMEM((128, B), BF16),
            pltpu.VMEM((128, B), BF16),
            pltpu.VMEM((128, K), BF16),
            pltpu.VMEM((NB, MAXB * 128, K), BF16),
            pltpu.VMEM((NB, K, MAXB * 128), BF16),
            pltpu.VMEM((NB, LEVD, 8, 128), F32),
            pltpu.VMEM((NB, MAXB * 128, COLD), BF16),
            dma((9,)),
            dma((NB,)),
            dma((2,)),
            dma((2,)),
            dma((2,)),
            dma((2,)),
            dma((NB,)),
            dma((NB,)),
            dma((NB,)),
            dma((NB,)),
            dma((NB,)),
            dma((NB,)),
        ],
        compiler_params=pltpu.CompilerParams(
            collective_id=0, has_side_effects=True, vmem_limit_bytes=48 * 2**20
        ),
    )(
        *(
            pltpu.with_memory_space_constraint(array, pltpu.HBM)
            for array in (
                state,
                jnp.swapaxes(prior, 1, 2),
                value,
                error,
                place,
                height,
                jnp.transpose(blocks, (2, 1, 0)),
                jnp.transpose(counts),
                loc,
                mask,
            )
        )
    )
    return analysis, jnp.swapaxes(post, 1, 2)


def solution(mesh):
    placed = (
        P("lev", None, "tile"),
        P(None, None, ("tile", "lev")),
        P(None, ("tile", "lev")),
        P(None, ("tile", "lev")),
        P(None, ("tile", "lev")),
        P(None, ("tile", "lev")),
        P(None, "tile", None),
        P(None, "tile"),
        P(None, None, "tile"),
        P(),
    )
    return jax.shard_map(
        per_device,
        mesh=mesh,
        in_specs=placed,
        out_specs=(P("lev", None, "tile"), P(None, None, ("tile", "lev"))),
        check_vma=False,
    )
```

```python
import math

import jax
import jax.numpy as jnp
from jax import lax
from jax.experimental import pallas as pl
from jax.experimental.pallas import tpu as pltpu
from jax.sharding import PartitionSpec as P

MESH = pl.DeviceIdType.MESH
F32 = jnp.float32
BF16 = jnp.bfloat16

K = 80
NB = 8
B = 2048
OBLK = 128
NOB = 16
MAXB = 6
LEVD = 8
COLD = 512
QUAD = 4
GRP = 8
OWN = OBLK // GRP

EPS = 1e-05
INV_REACH = 4.0
INV_VREACH = 0.125
COUPLE = 4.0 / math.sqrt(B) / (K - 1)
SCOUPLE = 4.0 / math.sqrt(MAXB * OBLK) / (K - 1)


def device(x, y, core, z):
    return ((x * 4 + y) * 2 + core, z)


def kernel(
    state_hbm,
    prior_hbm,
    value_hbm,
    error_hbm,
    place_hbm,
    height_hbm,
    blocks_hbm,
    counts_hbm,
    loc_hbm,
    mask_hbm,
    x_ref,
    post_ref,
    prior,
    vectors,
    blocks_ref,
    counts_ref,
    mine,
    piece,
    yo,
    yx,
    yt,
    aux,
    pcol,
    mrow,
    maskv,
    ab,
    st,
    hx,
    abc,
    vhc,
    rows,
    dyb,
    dys,
    near,
    rr,
    aet,
    abt,
    dch,
    scl,
    locv,
    in_sem,
    loc_sem,
    psend,
    precv,
    hsend,
    hrecv,
    ssend,
    srecv,
    bsend,
    brecv,
    ysend,
    yrecv,
):
    t = lax.axis_index("tile")
    z = lax.axis_index("lev")
    x, y, core = t // 8, (t // 2) % 4, t % 2
    own = x * 4 + y
    seat = core * 4 + z

    column = []
    for step in (4, 2, 6, 1, 3, 5, 7):
        other = lax.rem(seat + step, GRP)
        column.append(device(x, y, other // 4, lax.rem(other, 4)))
    hops = [(min(dx, 4 - dx) + min(dy, 4 - dy), dx, dy) for dx in range(4) for dy in range(4) if dx or dy]
    plane = []
    for _, dx, dy in sorted(hops, key=lambda hop: -hop[0]):
        plane.append(device(lax.rem(x + dx, 4), lax.rem(y + dy, 4), core, z))

    barrier = pltpu.get_barrier_semaphore()
    for peer in plane + column:
        pl.semaphore_signal(barrier, inc=1, device_id=peer, device_id_type=MESH)

    small = [
        pltpu.make_async_copy(src, dst, in_sem.at[i])
        for i, (src, dst) in enumerate(
            [
                (prior_hbm, prior),
                (value_hbm, vectors.at[0]),
                (error_hbm, vectors.at[1]),
                (place_hbm, vectors.at[2]),
                (height_hbm, vectors.at[3]),
                (mask_hbm.at[:, own], maskv),
                (blocks_hbm, blocks_ref),
                (counts_hbm, counts_ref),
                (state_hbm, x_ref),
            ]
        )
    ]
    for copy in small:
        copy.start()

    def load_loc(c):
        return pltpu.make_async_copy(loc_hbm.at[c], locv.at[c], loc_sem.at[c])

    for c in range(NB):
        load_loc(c).start()

    for copy in small[:5]:
        copy.wait()
    square = jnp.concatenate([vectors[g] for g in range(4)] + [jnp.zeros((128 - 4 * NB, OWN), F32)], axis=0)
    square = jnp.concatenate([square, jnp.zeros((128, 128 - OWN), F32)], axis=1)
    behind = jnp.transpose(square)[0:OWN, 0 : 128 - K]
    for e in range(NB):
        mine[e] = jnp.concatenate([prior[e], behind if e == 0 else jnp.zeros((OWN, 128 - K), F32)], axis=1)
    piece[seat, 0] = mine[0]
    piece[seat, 1] = mine[1]

    @pl.when(seat >= 2)
    def _():
        piece[seat, 2] = mine[seat]

    pl.semaphore_wait(barrier, len(column) + len(plane))

    def send(ref, send_sem, recv_sem, peers, target=None):
        for peer in peers:
            pltpu.make_async_remote_copy(
                src_ref=ref,
                dst_ref=ref if target is None else target,
                send_sem=send_sem,
                recv_sem=recv_sem,
                device_id=peer,
                device_id_type=MESH,
            ).start()

    def settle(ref, sem):
        pltpu.make_async_copy(ref, ref, sem).wait()

    send(mine.at[0], psend.at[0], precv.at[0], column, piece.at[seat, 0])

    small[5].wait()
    eye = lax.broadcasted_iota(jnp.int32, (NOB, NOB), 0) == lax.broadcasted_iota(jnp.int32, (NOB, NOB), 1)
    for e in range(1, NB):
        for c in range(e):
            chosen = jnp.where(eye, maskv[e, c : c + 1, :].astype(F32), 0.0)
            mrow[e, c] = jnp.broadcast_to(jnp.sum(chosen, axis=1, keepdims=True), (NOB, 128))

    def unpack(slot):
        return jnp.transpose(piece[:, slot].reshape(128, 128))

    settle(piece.at[pl.ds(0, GRP - 1), 0], precv.at[0])
    first = unpack(0)
    yo[0] = first[0:K]
    for g in range(4):
        aux[g] = first[K + g * NB : K + (g + 1) * NB] * (INV_REACH if g == 2 else 1.0)
    for e in range(NB):
        for g in range(1, 4):
            hx[own, e, g - 1 : g, :] = aux[g, e : e + 1, :]
        hx[own, e, 3:4, :] = jnp.zeros((1, 128), F32)

    def publish(e):
        now = yo[e]
        average = jnp.sum(now, axis=0, keepdims=True) * (1.0 / K)
        anomaly = now - average
        variance = jnp.sum(anomaly * anomaly, axis=0, keepdims=True) * (1.0 / (K - 1)) + EPS
        st[e, own, 0:1, :] = variance
        st[e, own, 1:2, :] = aux[0, pl.ds(e, 1), :] - average
        send(st.at[e, own], ssend.at[e], srecv.at[e], plane)
        ab[e, own] = anomaly.astype(BF16)
        send(ab.at[e, own], bsend.at[e], brecv.at[e], plane)

    def take(e, ref, sem):
        settle(ref.at[e, pl.ds(0, NOB - 1)], sem.at[e])

    send(hx.at[own, 0], hsend.at[0], hrecv.at[0], plane)
    publish(0)
    send(mine.at[1], psend.at[1], precv.at[1], column, piece.at[seat, 1])
    for e in range(2, NB):

        @pl.when(seat != e)
        def _():
            send(mine.at[e], psend.at[2], precv.at[2], [device(x, y, e // 4, e % 4)], piece.at[seat, 2])

    send(hx.at[own, pl.ds(1, NB - 1)], hsend.at[1], hrecv.at[1], plane)
    hx_first = hx.at[pl.ds(0, NOB - 1), 0]
    hx_rest = hx.at[pl.ds(0, NOB - 1), pl.ds(1, NB - 1)]
    settle(piece.at[pl.ds(0, GRP - 1), 1], precv.at[1])
    yo[1] = unpack(1)[0:K]

    @pl.when(seat >= 2)
    def _():
        settle(piece.at[pl.ds(0, GRP - 1), 2], precv.at[2])
        yo[seat] = unpack(2)[0:K]

    @pl.loop(0, NB)
    def _(e):
        pcol[e] = jnp.transpose(jnp.broadcast_to(aux[2, pl.ds(e, 1), :], (128, 128)))

    def nearness(c, e):
        mine = pcol[e]
        for b in range(NOB):
            cut = slice(b * 128, (b + 1) * 128)
            gap = mine - hx[b, c, 1:2, :]
            near[:, cut] = pl.reciprocal(1.0 + gap * gap, approx=True).astype(BF16)

    def transposed(e):
        now = yo[e]
        average = jnp.sum(now, axis=0, keepdims=True) * (1.0 / K)
        aet[...] = jnp.transpose(now - average).astype(BF16)

    def regress(c, e):
        for part in range(4):
            cut = slice(part * 512, (part + 1) * 512)
            theirs = jnp.concatenate(
                [ab[c, b] * mrow[e, c, b : b + 1, :].astype(BF16) for b in range(part * 4, part * 4 + 4)], axis=1
            )
            covar = jnp.dot(aet[...], theirs, preferred_element_type=F32)
            rr[:, cut] = covar.astype(BF16) * near[:, cut]
        yo[e] += lax.dot_general(dys[...], rr[...], (((1,), (1,)), ((), ())), preferred_element_type=F32)

    level = (lax.broadcasted_iota(jnp.int32, (LEVD, 128), 0) + z * LEVD).astype(F32) + 0.5

    for copy in small[6:]:
        copy.wait()
    settle(hx_first, hrecv.at[0])

    def state_quad(quad):
        c = quad // (LEVD // QUAD)
        start = (quad % (LEVD // QUAD)) * QUAD
        lows, results, gain = [], [], None
        for i in range(QUAD):
            block = x_ref[start + i]
            lows.append((block - jnp.sum(block, axis=0, keepdims=True) * (1.0 / K)).astype(BF16))
        for i in range(QUAD + 1):
            before = gain
            if i < QUAD:
                covar = jnp.dot(abt[c], lows[i], preferred_element_type=F32)
                gain = covar.astype(BF16) * locv[c]
            if i > 0:
                factors = [
                    (dch[c, :, j * 128 : (j + 1) * 128].astype(F32) * scl[c, start + i - 1, j : j + 1, :]).astype(BF16)
                    for j in range(MAXB)
                ]
                delta = jnp.concatenate(factors, axis=1)
                results.append(jnp.dot(delta, before, preferred_element_type=F32))
        for i in range(QUAD):
            x_ref[start + i] += results[i]

    @pl.loop(0, NB)
    def _(c):
        @pl.when(c == 1)
        def _():
            settle(hx_rest, hrecv.at[1])

        @pl.when((c >= 1) & (c < NB - 1))
        def _():
            @pl.when(seat == c + 1)
            def _():
                settle(yx.at[pl.ds(0, GRP - 1)], ysend.at[c + 1])

            @pl.when(seat != c + 1)
            def _():
                settle(yx.at[c + 1], yrecv.at[c + 1])
                yo[c + 1] = yx[c + 1]

        @pl.when(c < NB - 1)
        def _():
            transposed(c + 1)
            nearness(c, c + 1)

        take(c, st, srecv)
        variance, miss, error = st[c, :, 0, :], st[c, :, 1, :], hx[:, c, 0, :]
        gamma = jnp.sum(miss * miss, keepdims=True) / jnp.sum(variance + error, keepdims=True)
        inflated = gamma * variance
        both = inflated + error
        rows[0] = inflated / both * miss
        rows[1] = jnp.sqrt(gamma * error / both) - 1.0
        rows[2] = COUPLE / variance

        take(c, ab, brecv)

        def increments():
            for b in range(NOB):
                low = (rows[0, b : b + 1, :] + rows[1, b : b + 1, :] * ab[c, b].astype(F32)).astype(BF16)
                dyb[b] = low
                dys[:, b * 128 : (b + 1) * 128] = (low.astype(F32) * rows[2, b : b + 1, :]).astype(BF16)

        @pl.when(c < NB - 1)
        def _():
            increments()
            regress(c, c + 1)
            publish(c + 1)

        @pl.when(c == NB - 1)
        def _():
            increments()

        @pl.when((seat >= 2) & (seat >= c + 2))
        def _():
            transposed(seat)
            nearness(c, seat)
            regress(c, seat)

            @pl.when(seat == c + 2)
            def _():
                send(yo.at[seat], ysend.at[seat], yrecv.at[seat], column, yx.at[seat])

        abc[...] = ab[c]
        vhc[:, 0, :] = variance
        vhc[:, 1, :] = hx[:, c, 2, :]
        load_loc(c).wait()
        used = counts_ref[0, c]
        for i in range(MAXB):
            block = blocks_ref[i, 0, c]
            cut = slice(i * 128, (i + 1) * 128)
            abt[c, cut, :] = jnp.transpose(abc[block].astype(F32)).astype(BF16)
            dch[c, :, cut] = dyb[block]
            theirs = vhc[block]
            gap = (level - theirs[1:2, :]) * INV_VREACH
            weight = jnp.where(i < used, SCOUPLE, 0.0) / theirs[0:1, :]
            scl[c, :, i, :] = weight / (1.0 + gap * gap)

        pl.loop(c * (LEVD // QUAD), (c + 1) * (LEVD // QUAD))(state_quad)

        final = yo[c] + dyb[own].astype(F32)
        yt[...] = jnp.transpose(final)
        post_ref[c] = yt[pl.ds(pl.multiple_of(seat * OWN, OWN), OWN), :]

    settle(piece.at[pl.ds(0, GRP - 1), 0], psend.at[0])
    settle(piece.at[pl.ds(0, GRP - 1), 1], psend.at[1])

    @pl.when(seat >= 2)
    def _():
        settle(mine.at[pl.ds(0, NB - 3)], psend.at[2])

    @pl.when(seat < 2)
    def _():
        settle(mine.at[pl.ds(0, NB - 2)], psend.at[2])

    settle(hx_first, hsend.at[0])
    settle(hx_rest, hsend.at[1])

    @pl.loop(0, NB)
    def _(c):
        take(c, st, ssend)
        take(c, ab, bsend)


def per_device(state, prior, value, error, place, height, blocks, counts, loc, mask):
    vmem = pl.BlockSpec(memory_space=pltpu.VMEM)
    hbm = pl.BlockSpec(memory_space=pltpu.HBM)
    dma = pltpu.SemaphoreType.DMA
    analysis, post = pl.pallas_call(
        kernel,
        out_shape=(
            jax.ShapeDtypeStruct((LEVD, K, COLD), F32),
            jax.ShapeDtypeStruct((NB, OWN, K), F32),
        ),
        in_specs=[hbm] * 10,
        out_specs=(vmem, vmem),
        scratch_shapes=[
            pltpu.VMEM((NB, OWN, K), F32),
            pltpu.VMEM((4, NB, OWN), F32),
            pltpu.SMEM((MAXB, 1, NB), jnp.int32),
            pltpu.SMEM((1, NB), jnp.int32),
            pltpu.VMEM((NB, OWN, 128), F32),
            pltpu.VMEM((GRP, 3, OWN, 128), F32),
            pltpu.VMEM((NB, K, 128), F32),
            pltpu.VMEM((NB, K, 128), F32),
            pltpu.VMEM((128, K), F32),
            pltpu.VMEM((4, NB, 128), F32),
            pltpu.VMEM((NB, 128, 128), F32),
            pltpu.VMEM((NB, NB, NOB, 128), F32),
            pltpu.VMEM((NB, NB, NOB), jnp.int32),
            pltpu.VMEM((NB, NOB, K, 128), BF16),
            pltpu.VMEM((NB, NOB, 2, 128), F32),
            pltpu.VMEM((NOB, NB, 4, 128), F32),
            pltpu.VMEM((NOB, K, 128), BF16),
            pltpu.VMEM((NOB, 2, 128), F32),
            pltpu.VMEM((3, NOB, 128), F32),
            pltpu.VMEM((NOB, K, 128), BF16),
            pltpu.VMEM((K, B), BF16),
            pltpu.VMEM((128, B), BF16),
            pltpu.VMEM((128, B), BF16),
            pltpu.VMEM((128, K), BF16),
            pltpu.VMEM((NB, MAXB * 128, K), BF16),
            pltpu.VMEM((NB, K, MAXB * 128), BF16),
            pltpu.VMEM((NB, LEVD, 8, 128), F32),
            pltpu.VMEM((NB, MAXB * 128, COLD), BF16),
            dma((9,)),
            dma((NB,)),
            dma((3,)),
            dma((3,)),
            dma((2,)),
            dma((2,)),
            dma((NB,)),
            dma((NB,)),
            dma((NB,)),
            dma((NB,)),
            dma((NB,)),
            dma((NB,)),
        ],
        compiler_params=pltpu.CompilerParams(
            collective_id=0, has_side_effects=True, vmem_limit_bytes=48 * 2**20
        ),
    )(
        *(
            pltpu.with_memory_space_constraint(array, pltpu.HBM)
            for array in (
                state,
                jnp.swapaxes(prior, 1, 2),
                value,
                error,
                place,
                height,
                jnp.transpose(blocks, (2, 1, 0)),
                jnp.transpose(counts),
                loc,
                mask,
            )
        )
    )
    return analysis, jnp.swapaxes(post, 1, 2)


def solution(mesh):
    placed = (
        P("lev", None, "tile"),
        P(None, None, ("tile", "lev")),
        P(None, ("tile", "lev")),
        P(None, ("tile", "lev")),
        P(None, ("tile", "lev")),
        P(None, ("tile", "lev")),
        P(None, "tile", None),
        P(None, "tile"),
        P(None, None, "tile"),
        P(),
    )
    return jax.shard_map(
        per_device,
        mesh=mesh,
        in_specs=placed,
        out_specs=(P("lev", None, "tile"), P(None, None, ("tile", "lev"))),
        check_vma=False,
    )
```

```python
import math

import jax
import jax.numpy as jnp
from jax import lax
from jax.experimental import pallas as pl
from jax.experimental.pallas import tpu as pltpu
from jax.sharding import PartitionSpec as P

MESH = pl.DeviceIdType.MESH
F32 = jnp.float32
BF16 = jnp.bfloat16

K = 80
NB = 8
B = 2048
OBLK = 128
NOB = 16
MAXB = 6
LEVD = 8
COLD = 512
QUAD = 4
GRP = 8
OWN = OBLK // GRP

EPS = 1e-05
INV_REACH = 4.0
INV_VREACH = 0.125
COUPLE = 4.0 / math.sqrt(B) / (K - 1)
SCOUPLE = 4.0 / math.sqrt(MAXB * OBLK) / (K - 1)


def device(x, y, core, z):
    return ((x * 4 + y) * 2 + core, z)


def state_changes(x_ref, start, abt, dch, scl, loc, used=MAXB):
    listed = slice(0, used * OBLK)
    lows, results, gain = [], [], None
    for i in range(QUAD):
        block = x_ref[start + i]
        lows.append((block - jnp.sum(block, axis=0, keepdims=True) * (1.0 / K)).astype(BF16))
    for i in range(QUAD + 1):
        before = gain
        if i < QUAD:
            covar = jnp.dot(abt[listed, :], lows[i], preferred_element_type=F32)
            gain = covar.astype(BF16) * loc[listed, :]
        if i > 0:
            factors = [
                (dch[:, j * 128 : (j + 1) * 128].astype(F32) * scl[start + i - 1, j : j + 1, :]).astype(BF16)
                for j in range(used)
            ]
            delta = jnp.concatenate(factors, axis=1)
            results.append(jnp.dot(delta, before, preferred_element_type=F32))
    return results


def last_kernel(x_ref, post_ref, abt, dch, scl, loc, x_hbm, post_hbm, held, out_sem, post_sem):
    store_post = pltpu.make_async_copy(post_ref, post_hbm, post_sem)
    store_post.start()

    def store(l):
        return pltpu.make_async_copy(held.at[l], x_hbm.at[l], out_sem.at[l])

    count = jnp.max(scl[0, 7:8, :])
    for used in range(1, MAXB + 1):

        @pl.when((count > used - 0.5) & (count < used + 0.5))
        def _():
            @pl.loop(0, LEVD // QUAD)
            def _(h):
                results = state_changes(x_ref, h * QUAD, abt, dch, scl, loc, used)
                for i in range(QUAD):
                    held[h * QUAD + i] = x_ref[h * QUAD + i] + results[i]
                    store(h * QUAD + i).start()

    for l in range(LEVD):
        store(l).wait()
    store_post.wait()


def kernel(
    state_hbm,
    prior_hbm,
    value_hbm,
    error_hbm,
    place_hbm,
    height_hbm,
    blocks_hbm,
    counts_hbm,
    loc_hbm,
    mask_hbm,
    x_ref,
    post_ref,
    abt_last,
    dch_last,
    scl_last,
    loc_last,
    prior,
    vectors,
    blocks_ref,
    counts_ref,
    mine,
    piece,
    yo,
    yx,
    yt,
    aux,
    pcol,
    mrow,
    maskv,
    ab,
    st,
    hx,
    abc,
    vhc,
    rows,
    dyb,
    dys,
    near,
    rr,
    aet,
    abt,
    dch,
    scl,
    locv,
    in_sem,
    loc_sem,
    psend,
    precv,
    hsend,
    hrecv,
    ssend,
    srecv,
    bsend,
    brecv,
    ysend,
    yrecv,
):
    t = lax.axis_index("tile")
    z = lax.axis_index("lev")
    x, y, core = t // 8, (t // 2) % 4, t % 2
    own = x * 4 + y
    seat = core * 4 + z

    column = []
    for step in (4, 2, 6, 1, 3, 5, 7):
        other = lax.rem(seat + step, GRP)
        column.append(device(x, y, other // 4, lax.rem(other, 4)))
    hops = [(min(dx, 4 - dx) + min(dy, 4 - dy), dx, dy) for dx in range(4) for dy in range(4) if dx or dy]
    plane = []
    for _, dx, dy in sorted(hops, key=lambda hop: -hop[0]):
        plane.append(device(lax.rem(x + dx, 4), lax.rem(y + dy, 4), core, z))

    barrier = pltpu.get_barrier_semaphore()
    for peer in plane + column:
        pl.semaphore_signal(barrier, inc=1, device_id=peer, device_id_type=MESH)

    small = [
        pltpu.make_async_copy(src, dst, in_sem.at[i])
        for i, (src, dst) in enumerate(
            [
                (prior_hbm, prior),
                (value_hbm, vectors.at[0]),
                (error_hbm, vectors.at[1]),
                (place_hbm, vectors.at[2]),
                (height_hbm, vectors.at[3]),
                (mask_hbm.at[:, own], maskv),
                (blocks_hbm, blocks_ref),
                (counts_hbm, counts_ref),
                (state_hbm, x_ref),
            ]
        )
    ]
    for copy in small:
        copy.start()

    def load_loc(c):
        return pltpu.make_async_copy(loc_hbm.at[c], locv.at[c], loc_sem.at[c])

    load_last = pltpu.make_async_copy(loc_hbm.at[NB - 1], loc_last, loc_sem.at[NB - 1])
    for c in range(NB - 1):
        load_loc(c).start()
    load_last.start()

    for copy in small[:5]:
        copy.wait()
    square = jnp.concatenate([vectors[g] for g in range(4)] + [jnp.zeros((128 - 4 * NB, OWN), F32)], axis=0)
    square = jnp.concatenate([square, jnp.zeros((128, 128 - OWN), F32)], axis=1)
    behind = jnp.transpose(square)[0:OWN, 0 : 128 - K]
    for e in range(NB):
        mine[e] = jnp.concatenate([prior[e], behind if e == 0 else jnp.zeros((OWN, 128 - K), F32)], axis=1)
    piece[seat, 0] = mine[0]
    piece[seat, 1] = mine[1]

    @pl.when(seat >= 2)
    def _():
        piece[seat, 2] = mine[seat]

    pl.semaphore_wait(barrier, len(column) + len(plane))

    def send(ref, send_sem, recv_sem, peers, target=None):
        for peer in peers:
            pltpu.make_async_remote_copy(
                src_ref=ref,
                dst_ref=ref if target is None else target,
                send_sem=send_sem,
                recv_sem=recv_sem,
                device_id=peer,
                device_id_type=MESH,
            ).start()

    def settle(ref, sem):
        pltpu.make_async_copy(ref, ref, sem).wait()

    send(mine.at[0], psend.at[0], precv.at[0], column, piece.at[seat, 0])

    small[5].wait()
    eye = lax.broadcasted_iota(jnp.int32, (NOB, NOB), 0) == lax.broadcasted_iota(jnp.int32, (NOB, NOB), 1)
    for e in range(1, NB):
        for c in range(e):
            chosen = jnp.where(eye, maskv[e, c : c + 1, :].astype(F32), 0.0)
            mrow[e, c] = jnp.broadcast_to(jnp.sum(chosen, axis=1, keepdims=True), (NOB, 128))

    def unpack(slot):
        return jnp.transpose(piece[:, slot].reshape(128, 128))

    settle(piece.at[pl.ds(0, GRP - 1), 0], precv.at[0])
    first = unpack(0)
    yo[0] = first[0:K]
    for g in range(4):
        aux[g] = first[K + g * NB : K + (g + 1) * NB] * (INV_REACH if g == 2 else 1.0)
    for e in range(NB):
        for g in range(1, 4):
            hx[own, e, g - 1 : g, :] = aux[g, e : e + 1, :]
        hx[own, e, 3:4, :] = jnp.zeros((1, 128), F32)

    def publish(e):
        now = yo[e]
        average = jnp.sum(now, axis=0, keepdims=True) * (1.0 / K)
        anomaly = now - average
        variance = jnp.sum(anomaly * anomaly, axis=0, keepdims=True) * (1.0 / (K - 1)) + EPS
        st[e, own, 0:1, :] = variance
        st[e, own, 1:2, :] = aux[0, pl.ds(e, 1), :] - average
        send(st.at[e, own], ssend.at[e], srecv.at[e], plane)
        ab[e, own] = anomaly.astype(BF16)
        send(ab.at[e, own], bsend.at[e], brecv.at[e], plane)

    def take(e, ref, sem):
        settle(ref.at[e, pl.ds(0, NOB - 1)], sem.at[e])

    send(hx.at[own, 0], hsend.at[0], hrecv.at[0], plane)
    publish(0)
    send(mine.at[1], psend.at[1], precv.at[1], column, piece.at[seat, 1])
    for e in range(2, NB):

        @pl.when(seat != e)
        def _():
            send(mine.at[e], psend.at[2], precv.at[2], [device(x, y, e // 4, e % 4)], piece.at[seat, 2])

    send(hx.at[own, pl.ds(1, NB - 1)], hsend.at[1], hrecv.at[1], plane)
    hx_first = hx.at[pl.ds(0, NOB - 1), 0]
    hx_rest = hx.at[pl.ds(0, NOB - 1), pl.ds(1, NB - 1)]
    settle(piece.at[pl.ds(0, GRP - 1), 1], precv.at[1])
    yo[1] = unpack(1)[0:K]

    @pl.when(seat >= 2)
    def _():
        settle(piece.at[pl.ds(0, GRP - 1), 2], precv.at[2])
        yo[seat] = unpack(2)[0:K]

    @pl.loop(0, NB)
    def _(e):
        pcol[e] = jnp.transpose(jnp.broadcast_to(aux[2, pl.ds(e, 1), :], (128, 128)))

    def nearness(c, e):
        mine = pcol[e]
        for b in range(NOB):
            cut = slice(b * 128, (b + 1) * 128)
            gap = mine - hx[b, c, 1:2, :]
            near[:, cut] = pl.reciprocal(1.0 + gap * gap, approx=True).astype(BF16)

    def transposed(e):
        now = yo[e]
        average = jnp.sum(now, axis=0, keepdims=True) * (1.0 / K)
        aet[...] = jnp.transpose(now - average).astype(BF16)

    def regress(c, e):
        for part in range(4):
            cut = slice(part * 512, (part + 1) * 512)
            theirs = jnp.concatenate(
                [ab[c, b] * mrow[e, c, b : b + 1, :].astype(BF16) for b in range(part * 4, part * 4 + 4)], axis=1
            )
            covar = jnp.dot(aet[...], theirs, preferred_element_type=F32)
            rr[:, cut] = covar.astype(BF16) * near[:, cut]
        yo[e] += lax.dot_general(dys[...], rr[...], (((1,), (1,)), ((), ())), preferred_element_type=F32)

    level = (lax.broadcasted_iota(jnp.int32, (LEVD, 128), 0) + z * LEVD).astype(F32) + 0.5

    for copy in small[6:]:
        copy.wait()
    scl[NB - 1] = jnp.full((LEVD, 8, 128), counts_ref[0, NB - 1].astype(F32))
    settle(hx_first, hrecv.at[0])

    def state_quad(quad):
        c = quad // (LEVD // QUAD)
        start = (quad % (LEVD // QUAD)) * QUAD
        results = state_changes(x_ref, start, abt.at[c], dch.at[c], scl.at[c], locv.at[c])
        for i in range(QUAD):
            x_ref[start + i] += results[i]

    @pl.loop(0, NB)
    def _(c):
        @pl.when(c == 1)
        def _():
            settle(hx_rest, hrecv.at[1])

        @pl.when((c >= 1) & (c < NB - 1))
        def _():
            @pl.when(seat == c + 1)
            def _():
                settle(yx.at[pl.ds(0, GRP - 1)], ysend.at[c + 1])

            @pl.when(seat != c + 1)
            def _():
                settle(yx.at[c + 1], yrecv.at[c + 1])
                yo[c + 1] = yx[c + 1]

        @pl.when(c < NB - 1)
        def _():
            transposed(c + 1)
            nearness(c, c + 1)

        take(c, st, srecv)
        variance, miss, error = st[c, :, 0, :], st[c, :, 1, :], hx[:, c, 0, :]
        gamma = jnp.sum(miss * miss, keepdims=True) / jnp.sum(variance + error, keepdims=True)
        inflated = gamma * variance
        both = inflated + error
        rows[0] = inflated / both * miss
        rows[1] = jnp.sqrt(gamma * error / both) - 1.0
        rows[2] = COUPLE / variance

        take(c, ab, brecv)

        def increments():
            for b in range(NOB):
                low = (rows[0, b : b + 1, :] + rows[1, b : b + 1, :] * ab[c, b].astype(F32)).astype(BF16)
                dyb[b] = low
                dys[:, b * 128 : (b + 1) * 128] = (low.astype(F32) * rows[2, b : b + 1, :]).astype(BF16)

        @pl.when(c < NB - 1)
        def _():
            increments()
            regress(c, c + 1)
            publish(c + 1)

        @pl.when(c == NB - 1)
        def _():
            increments()

        @pl.when((seat >= 2) & (seat >= c + 2))
        def _():
            transposed(seat)
            nearness(c, seat)
            regress(c, seat)

            @pl.when(seat == c + 2)
            def _():
                send(yo.at[seat], ysend.at[seat], yrecv.at[seat], column, yx.at[seat])

        abc[...] = ab[c]
        vhc[:, 0, :] = variance
        vhc[:, 1, :] = hx[:, c, 2, :]
        used = counts_ref[0, c]
        for i in range(MAXB):
            block = blocks_ref[i, 0, c]
            cut = slice(i * 128, (i + 1) * 128)
            abt[c, cut, :] = jnp.transpose(abc[block].astype(F32)).astype(BF16)
            dch[c, :, cut] = dyb[block]
            theirs = vhc[block]
            gap = (level - theirs[1:2, :]) * INV_VREACH
            weight = jnp.where(i < used, SCOUPLE, 0.0) / theirs[0:1, :]
            scl[c, :, i, :] = weight / (1.0 + gap * gap)

        @pl.when(c < NB - 1)
        def _():
            load_loc(c).wait()
            pl.loop(c * (LEVD // QUAD), (c + 1) * (LEVD // QUAD))(state_quad)

        final = yo[c] + dyb[own].astype(F32)
        yt[...] = jnp.transpose(final)
        post_ref[c] = yt[pl.ds(pl.multiple_of(seat * OWN, OWN), OWN), :]

    abt_last[...] = abt[NB - 1]
    dch_last[...] = dch[NB - 1]
    scl_last[...] = scl[NB - 1]
    load_last.wait()
    settle(piece.at[pl.ds(0, GRP - 1), 0], psend.at[0])
    settle(piece.at[pl.ds(0, GRP - 1), 1], psend.at[1])

    @pl.when(seat >= 2)
    def _():
        settle(mine.at[pl.ds(0, NB - 3)], psend.at[2])

    @pl.when(seat < 2)
    def _():
        settle(mine.at[pl.ds(0, NB - 2)], psend.at[2])

    settle(hx_first, hsend.at[0])
    settle(hx_rest, hsend.at[1])

    @pl.loop(0, NB)
    def _(c):
        take(c, st, ssend)
        take(c, ab, bsend)


def per_device(state, prior, value, error, place, height, blocks, counts, loc, mask):
    vmem = pl.BlockSpec(memory_space=pltpu.VMEM)
    hbm = pl.BlockSpec(memory_space=pltpu.HBM)
    dma = pltpu.SemaphoreType.DMA
    carried = pl.pallas_call(
        kernel,
        out_shape=(
            jax.ShapeDtypeStruct((LEVD, K, COLD), F32),
            jax.ShapeDtypeStruct((NB, OWN, K), F32),
            jax.ShapeDtypeStruct((MAXB * 128, K), BF16),
            jax.ShapeDtypeStruct((K, MAXB * 128), BF16),
            jax.ShapeDtypeStruct((LEVD, 8, 128), F32),
            jax.ShapeDtypeStruct((MAXB * 128, COLD), BF16),
        ),
        in_specs=[hbm] * 10,
        out_specs=(vmem,) * 6,
        scratch_shapes=[
            pltpu.VMEM((NB, OWN, K), F32),
            pltpu.VMEM((4, NB, OWN), F32),
            pltpu.SMEM((MAXB, 1, NB), jnp.int32),
            pltpu.SMEM((1, NB), jnp.int32),
            pltpu.VMEM((NB, OWN, 128), F32),
            pltpu.VMEM((GRP, 3, OWN, 128), F32),
            pltpu.VMEM((NB, K, 128), F32),
            pltpu.VMEM((NB, K, 128), F32),
            pltpu.VMEM((128, K), F32),
            pltpu.VMEM((4, NB, 128), F32),
            pltpu.VMEM((NB, 128, 128), F32),
            pltpu.VMEM((NB, NB, NOB, 128), F32),
            pltpu.VMEM((NB, NB, NOB), jnp.int32),
            pltpu.VMEM((NB, NOB, K, 128), BF16),
            pltpu.VMEM((NB, NOB, 2, 128), F32),
            pltpu.VMEM((NOB, NB, 4, 128), F32),
            pltpu.VMEM((NOB, K, 128), BF16),
            pltpu.VMEM((NOB, 2, 128), F32),
            pltpu.VMEM((3, NOB, 128), F32),
            pltpu.VMEM((NOB, K, 128), BF16),
            pltpu.VMEM((K, B), BF16),
            pltpu.VMEM((128, B), BF16),
            pltpu.VMEM((128, B), BF16),
            pltpu.VMEM((128, K), BF16),
            pltpu.VMEM((NB, MAXB * 128, K), BF16),
            pltpu.VMEM((NB, K, MAXB * 128), BF16),
            pltpu.VMEM((NB, LEVD, 8, 128), F32),
            pltpu.VMEM((NB - 1, MAXB * 128, COLD), BF16),
            dma((9,)),
            dma((NB,)),
            dma((3,)),
            dma((3,)),
            dma((2,)),
            dma((2,)),
            dma((NB,)),
            dma((NB,)),
            dma((NB,)),
            dma((NB,)),
            dma((NB,)),
            dma((NB,)),
        ],
        compiler_params=pltpu.CompilerParams(
            collective_id=0, has_side_effects=True, vmem_limit_bytes=32 * 2**20
        ),
    )(
        *(
            pltpu.with_memory_space_constraint(array, pltpu.HBM)
            for array in (
                state,
                jnp.swapaxes(prior, 1, 2),
                value,
                error,
                place,
                height,
                jnp.transpose(blocks, (2, 1, 0)),
                jnp.transpose(counts),
                loc,
                mask,
            )
        )
    )
    analysis, post = pl.pallas_call(
        last_kernel,
        out_shape=(pltpu.HBM((LEVD, K, COLD), F32), pltpu.HBM((NB, OWN, K), F32)),
        in_specs=[vmem] * 6,
        out_specs=(hbm, hbm),
        scratch_shapes=[pltpu.VMEM((LEVD, K, COLD), F32), dma((LEVD,)), dma(())],
        compiler_params=pltpu.CompilerParams(vmem_limit_bytes=32 * 2**20),
    )(*carried)
    return analysis, jnp.swapaxes(post, 1, 2)


def solution(mesh):
    placed = (
        P("lev", None, "tile"),
        P(None, None, ("tile", "lev")),
        P(None, ("tile", "lev")),
        P(None, ("tile", "lev")),
        P(None, ("tile", "lev")),
        P(None, ("tile", "lev")),
        P(None, "tile", None),
        P(None, "tile"),
        P(None, None, "tile"),
        P(),
    )
    return jax.shard_map(
        per_device,
        mesh=mesh,
        in_specs=placed,
        out_specs=(P("lev", None, "tile"), P(None, None, ("tile", "lev"))),
        check_vma=False,
    )
```

```python
import math

import jax
import jax.numpy as jnp
from jax import lax
from jax.experimental import pallas as pl
from jax.experimental.pallas import tpu as pltpu
from jax.sharding import PartitionSpec as P

MESH = pl.DeviceIdType.MESH
F32 = jnp.float32
BF16 = jnp.bfloat16

K = 80
NB = 8
B = 2048
OBLK = 128
NOB = 16
MAXB = 6
LEVD = 8
COLD = 512
QUAD = 4
GRP = 8
OWN = OBLK // GRP

EPS = 1e-05
INV_REACH = 4.0
INV_VREACH = 0.125
COUPLE = 4.0 / math.sqrt(B) / (K - 1)
SCOUPLE = 4.0 / math.sqrt(MAXB * OBLK) / (K - 1)


def device(x, y, core, z):
    return ((x * 4 + y) * 2 + core, z)


def state_changes(x_ref, start, abt, dch, scl, loc, used=MAXB):
    listed = slice(0, used * OBLK)
    lows, results, gain = [], [], None
    for i in range(QUAD):
        block = x_ref[start + i]
        lows.append((block - jnp.sum(block, axis=0, keepdims=True) * (1.0 / K)).astype(BF16))
    for i in range(QUAD + 1):
        before = gain
        if i < QUAD:
            covar = jnp.dot(abt[listed, :], lows[i], preferred_element_type=F32)
            gain = covar.astype(BF16) * loc[listed, :]
        if i > 0:
            factors = [
                (dch[:, j * 128 : (j + 1) * 128].astype(F32) * scl[start + i - 1, j : j + 1, :]).astype(BF16)
                for j in range(used)
            ]
            delta = jnp.concatenate(factors, axis=1)
            results.append(jnp.dot(delta, before, preferred_element_type=F32))
    return results


def last_kernel(x_ref, post_ref, abt, dch, scl, loc, x_hbm, post_hbm, held, out_sem, post_sem):
    store_post = pltpu.make_async_copy(post_ref, post_hbm, post_sem)
    store_post.start()

    def store(l):
        return pltpu.make_async_copy(held.at[l], x_hbm.at[l], out_sem.at[l])

    count = jnp.max(scl[0, 7:8, :])
    for used in range(1, MAXB + 1):

        @pl.when((count > used - 0.5) & (count < used + 0.5))
        def _():
            @pl.loop(0, LEVD // QUAD)
            def _(h):
                results = state_changes(x_ref, h * QUAD, abt, dch, scl, loc, used)
                for i in range(QUAD):
                    held[h * QUAD + i] = x_ref[h * QUAD + i] + results[i]
                    store(h * QUAD + i).start()

    for l in range(LEVD):
        store(l).wait()
    store_post.wait()


def kernel(
    state_hbm,
    prior_hbm,
    value_hbm,
    error_hbm,
    place_hbm,
    height_hbm,
    blocks_hbm,
    counts_hbm,
    loc_hbm,
    mask_hbm,
    x_ref,
    post_ref,
    abt_last,
    dch_last,
    scl_last,
    loc_last,
    prior,
    vectors,
    blocks_ref,
    counts_ref,
    mine,
    piece,
    yo,
    yx,
    yt,
    aux,
    pcol,
    mrow,
    maskv,
    ab,
    st,
    hx,
    abc,
    vhc,
    rows,
    dyb,
    dys,
    near,
    rr,
    aet,
    abt,
    dch,
    scl,
    locv,
    in_sem,
    loc_sem,
    psend,
    precv,
    hsend,
    hrecv,
    ssend,
    srecv,
    bsend,
    brecv,
    ysend,
    yrecv,
):
    t = lax.axis_index("tile")
    z = lax.axis_index("lev")
    x, y, core = t // 8, (t // 2) % 4, t % 2
    own = x * 4 + y
    seat = core * 4 + z

    column = []
    for step in (4, 2, 6, 1, 3, 5, 7):
        other = lax.rem(seat + step, GRP)
        column.append(device(x, y, other // 4, lax.rem(other, 4)))
    hops = [(min(dx, 4 - dx) + min(dy, 4 - dy), dx, dy) for dx in range(4) for dy in range(4) if dx or dy]
    plane = []
    for _, dx, dy in sorted(hops, key=lambda hop: -hop[0]):
        plane.append(device(lax.rem(x + dx, 4), lax.rem(y + dy, 4), core, z))

    barrier = pltpu.get_barrier_semaphore()
    for peer in plane + column:
        pl.semaphore_signal(barrier, inc=1, device_id=peer, device_id_type=MESH)

    small = [
        pltpu.make_async_copy(src, dst, in_sem.at[i])
        for i, (src, dst) in enumerate(
            [
                (prior_hbm, prior),
                (value_hbm, vectors.at[0]),
                (error_hbm, vectors.at[1]),
                (place_hbm, vectors.at[2]),
                (height_hbm, vectors.at[3]),
                (mask_hbm.at[:, own], maskv),
                (blocks_hbm, blocks_ref),
                (counts_hbm, counts_ref),
                (state_hbm, x_ref),
            ]
        )
    ]
    for copy in small:
        copy.start()

    def load_loc(c):
        return pltpu.make_async_copy(loc_hbm.at[c], locv.at[c], loc_sem.at[c])

    load_last = pltpu.make_async_copy(loc_hbm.at[NB - 1], loc_last, loc_sem.at[NB - 1])
    for c in range(NB - 1):
        load_loc(c).start()
    load_last.start()

    for copy in small[:5]:
        copy.wait()
    square = jnp.concatenate([vectors[g] for g in range(4)] + [jnp.zeros((128 - 4 * NB, OWN), F32)], axis=0)
    square = jnp.concatenate([square, jnp.zeros((128, 128 - OWN), F32)], axis=1)
    behind = jnp.transpose(square)[0:OWN, 0 : 128 - K]
    for e in range(NB):
        mine[e] = jnp.concatenate([prior[e], behind if e == 0 else jnp.zeros((OWN, 128 - K), F32)], axis=1)
    piece[seat, 0] = mine[0]
    piece[seat, 1] = mine[1]

    @pl.when(seat >= 2)
    def _():
        piece[seat, 2] = mine[seat]

    pl.semaphore_wait(barrier, len(column) + len(plane))

    def send(ref, send_sem, recv_sem, peers, target=None):
        for peer in peers:
            pltpu.make_async_remote_copy(
                src_ref=ref,
                dst_ref=ref if target is None else target,
                send_sem=send_sem,
                recv_sem=recv_sem,
                device_id=peer,
                device_id_type=MESH,
            ).start()

    def settle(ref, sem):
        pltpu.make_async_copy(ref, ref, sem).wait()

    send(mine.at[0], psend.at[0], precv.at[0], column, piece.at[seat, 0])

    small[5].wait()
    eye = lax.broadcasted_iota(jnp.int32, (NOB, NOB), 0) == lax.broadcasted_iota(jnp.int32, (NOB, NOB), 1)
    for e in range(1, NB):
        for c in range(e):
            chosen = jnp.where(eye, maskv[e, c : c + 1, :].astype(F32), 0.0)
            mrow[e, c] = jnp.broadcast_to(jnp.sum(chosen, axis=1, keepdims=True), (NOB, 128))

    def unpack(slot):
        return jnp.transpose(piece[:, slot].reshape(128, 128))

    settle(piece.at[pl.ds(0, GRP - 1), 0], precv.at[0])
    first = unpack(0)
    yo[0] = first[0:K]
    for g in range(4):
        aux[g] = first[K + g * NB : K + (g + 1) * NB] * (INV_REACH if g == 2 else 1.0)
    for e in range(NB):
        for g in range(1, 4):
            hx[own, e, g - 1 : g, :] = aux[g, e : e + 1, :]
        hx[own, e, 3:4, :] = jnp.zeros((1, 128), F32)

    def publish(e):
        now = yo[e]
        average = jnp.sum(now, axis=0, keepdims=True) * (1.0 / K)
        anomaly = now - average
        variance = jnp.sum(anomaly * anomaly, axis=0, keepdims=True) * (1.0 / (K - 1)) + EPS
        st[e, own, 0:1, :] = variance
        st[e, own, 1:2, :] = aux[0, pl.ds(e, 1), :] - average
        send(st.at[e, own], ssend.at[e], srecv.at[e], plane)
        ab[e, own] = anomaly.astype(BF16)
        send(ab.at[e, own], bsend.at[e], brecv.at[e], plane)

    def take(e, ref, sem):
        settle(ref.at[e, pl.ds(0, NOB - 1)], sem.at[e])

    send(hx.at[own, 0], hsend.at[0], hrecv.at[0], plane)
    publish(0)
    send(mine.at[1], psend.at[1], precv.at[1], column, piece.at[seat, 1])
    for e in range(2, NB):

        @pl.when(seat != e)
        def _():
            send(mine.at[e], psend.at[2], precv.at[2], [device(x, y, e // 4, e % 4)], piece.at[seat, 2])

    send(hx.at[own, pl.ds(1, NB - 1)], hsend.at[1], hrecv.at[1], plane)
    hx_first = hx.at[pl.ds(0, NOB - 1), 0]
    hx_rest = hx.at[pl.ds(0, NOB - 1), pl.ds(1, NB - 1)]
    settle(piece.at[pl.ds(0, GRP - 1), 1], precv.at[1])
    yo[1] = unpack(1)[0:K]

    @pl.when(seat >= 2)
    def _():
        settle(piece.at[pl.ds(0, GRP - 1), 2], precv.at[2])
        yo[seat] = unpack(2)[0:K]

    @pl.loop(0, NB)
    def _(e):
        pcol[e] = jnp.transpose(jnp.broadcast_to(aux[2, pl.ds(e, 1), :], (128, 128)))

    def nearness(c, e):
        mine = pcol[e]
        for b in range(NOB):
            cut = slice(b * 128, (b + 1) * 128)
            gap = mine - hx[b, c, 1:2, :]
            near[:, cut] = pl.reciprocal(1.0 + gap * gap, approx=True).astype(BF16)

    def transposed(e):
        now = yo[e]
        average = jnp.sum(now, axis=0, keepdims=True) * (1.0 / K)
        aet[...] = jnp.transpose(now - average).astype(BF16)

    def regress(c, e):
        for part in range(4):
            cut = slice(part * 512, (part + 1) * 512)
            theirs = jnp.concatenate(
                [ab[c, b] * mrow[e, c, b : b + 1, :].astype(BF16) for b in range(part * 4, part * 4 + 4)], axis=1
            )
            covar = jnp.dot(aet[...], theirs, preferred_element_type=F32)
            rr[:, cut] = covar.astype(BF16) * near[:, cut]
        yo[e] += lax.dot_general(dys[...], rr[...], (((1,), (1,)), ((), ())), preferred_element_type=F32)

    level = (lax.broadcasted_iota(jnp.int32, (LEVD, 128), 0) + z * LEVD).astype(F32) + 0.5

    for copy in small[6:]:
        copy.wait()
    scl_last[...] = jnp.full((LEVD, 8, 128), counts_ref[0, NB - 1].astype(F32))
    settle(hx_first, hrecv.at[0])

    def state_quad(quad):
        c = quad // (LEVD // QUAD)
        start = (quad % (LEVD // QUAD)) * QUAD
        results = state_changes(x_ref, start, abt.at[c], dch.at[c], scl.at[c], locv.at[c])
        for i in range(QUAD):
            x_ref[start + i] += results[i]

    @pl.loop(0, NB)
    def _(c):
        @pl.when(c == 1)
        def _():
            settle(hx_rest, hrecv.at[1])

        @pl.when((c >= 1) & (c < NB - 1))
        def _():
            @pl.when(seat == c + 1)
            def _():
                settle(yx.at[pl.ds(0, GRP - 1)], ysend.at[c + 1])

            @pl.when(seat != c + 1)
            def _():
                settle(yx.at[c + 1], yrecv.at[c + 1])
                yo[c + 1] = yx[c + 1]

        @pl.when(c < NB - 1)
        def _():
            transposed(c + 1)
            nearness(c, c + 1)

        take(c, st, srecv)
        variance, miss, error = st[c, :, 0, :], st[c, :, 1, :], hx[:, c, 0, :]
        gamma = jnp.sum(miss * miss, keepdims=True) / jnp.sum(variance + error, keepdims=True)
        inflated = gamma * variance
        both = inflated + error
        rows[0] = inflated / both * miss
        rows[1] = jnp.sqrt(gamma * error / both) - 1.0
        rows[2] = COUPLE / variance

        take(c, ab, brecv)

        def increments(scaled):
            for b in range(NOB):
                low = (rows[0, b : b + 1, :] + rows[1, b : b + 1, :] * ab[c, b].astype(F32)).astype(BF16)
                dyb[b] = low
                if scaled:
                    dys[:, b * 128 : (b + 1) * 128] = (low.astype(F32) * rows[2, b : b + 1, :]).astype(BF16)

        @pl.when(c < NB - 1)
        def _():
            increments(True)
            regress(c, c + 1)
            publish(c + 1)

        @pl.when(c == NB - 1)
        def _():
            increments(False)

        @pl.when((seat >= 2) & (seat >= c + 2))
        def _():
            transposed(seat)
            nearness(c, seat)
            regress(c, seat)

            @pl.when(seat == c + 2)
            def _():
                send(yo.at[seat], ysend.at[seat], yrecv.at[seat], column, yx.at[seat])

        abc[...] = ab[c]
        vhc[:, 0, :] = variance
        vhc[:, 1, :] = hx[:, c, 2, :]
        def prepare(turned, deltas, weights):
            used = counts_ref[0, c]
            for i in range(MAXB):
                block = blocks_ref[i, 0, c]
                cut = slice(i * 128, (i + 1) * 128)
                turned[cut, :] = jnp.transpose(abc[block].astype(F32)).astype(BF16)
                deltas[:, cut] = dyb[block]
                theirs = vhc[block]
                gap = (level - theirs[1:2, :]) * INV_VREACH
                weight = jnp.where(i < used, SCOUPLE, 0.0) / theirs[0:1, :]
                weights[:, i, :] = weight / (1.0 + gap * gap)

        @pl.when(c == NB - 1)
        def _():
            prepare(abt_last, dch_last, scl_last)

        @pl.when(c < NB - 1)
        def _():
            prepare(abt.at[c], dch.at[c], scl.at[c])

        @pl.when(c < NB - 1)
        def _():
            load_loc(c).wait()
            pl.loop(c * (LEVD // QUAD), (c + 1) * (LEVD // QUAD))(state_quad)

        final = yo[c] + dyb[own].astype(F32)
        yt[...] = jnp.transpose(final)
        post_ref[c] = yt[pl.ds(pl.multiple_of(seat * OWN, OWN), OWN), :]

    load_last.wait()
    settle(piece.at[pl.ds(0, GRP - 1), 0], psend.at[0])
    settle(piece.at[pl.ds(0, GRP - 1), 1], psend.at[1])

    @pl.when(seat >= 2)
    def _():
        settle(mine.at[pl.ds(0, NB - 3)], psend.at[2])

    @pl.when(seat < 2)
    def _():
        settle(mine.at[pl.ds(0, NB - 2)], psend.at[2])

    settle(hx_first, hsend.at[0])
    settle(hx_rest, hsend.at[1])

    @pl.loop(0, NB)
    def _(c):
        take(c, st, ssend)
        take(c, ab, bsend)


def per_device(state, prior, value, error, place, height, blocks, counts, loc, mask):
    vmem = pl.BlockSpec(memory_space=pltpu.VMEM)
    hbm = pl.BlockSpec(memory_space=pltpu.HBM)
    dma = pltpu.SemaphoreType.DMA
    carried = pl.pallas_call(
        kernel,
        out_shape=(
            jax.ShapeDtypeStruct((LEVD, K, COLD), F32),
            jax.ShapeDtypeStruct((NB, OWN, K), F32),
            jax.ShapeDtypeStruct((MAXB * 128, K), BF16),
            jax.ShapeDtypeStruct((K, MAXB * 128), BF16),
            jax.ShapeDtypeStruct((LEVD, 8, 128), F32),
            jax.ShapeDtypeStruct((MAXB * 128, COLD), BF16),
        ),
        in_specs=[hbm] * 10,
        out_specs=(vmem,) * 6,
        scratch_shapes=[
            pltpu.VMEM((NB, OWN, K), F32),
            pltpu.VMEM((4, NB, OWN), F32),
            pltpu.SMEM((MAXB, 1, NB), jnp.int32),
            pltpu.SMEM((1, NB), jnp.int32),
            pltpu.VMEM((NB, OWN, 128), F32),
            pltpu.VMEM((GRP, 3, OWN, 128), F32),
            pltpu.VMEM((NB, K, 128), F32),
            pltpu.VMEM((NB, K, 128), F32),
            pltpu.VMEM((128, K), F32),
            pltpu.VMEM((4, NB, 128), F32),
            pltpu.VMEM((NB, 128, 128), F32),
            pltpu.VMEM((NB, NB, NOB, 128), F32),
            pltpu.VMEM((NB, NB, NOB), jnp.int32),
            pltpu.VMEM((NB, NOB, K, 128), BF16),
            pltpu.VMEM((NB, NOB, 2, 128), F32),
            pltpu.VMEM((NOB, NB, 4, 128), F32),
            pltpu.VMEM((NOB, K, 128), BF16),
            pltpu.VMEM((NOB, 2, 128), F32),
            pltpu.VMEM((3, NOB, 128), F32),
            pltpu.VMEM((NOB, K, 128), BF16),
            pltpu.VMEM((K, B), BF16),
            pltpu.VMEM((128, B), BF16),
            pltpu.VMEM((128, B), BF16),
            pltpu.VMEM((128, K), BF16),
            pltpu.VMEM((NB, MAXB * 128, K), BF16),
            pltpu.VMEM((NB, K, MAXB * 128), BF16),
            pltpu.VMEM((NB, LEVD, 8, 128), F32),
            pltpu.VMEM((NB - 1, MAXB * 128, COLD), BF16),
            dma((9,)),
            dma((NB,)),
            dma((3,)),
            dma((3,)),
            dma((2,)),
            dma((2,)),
            dma((NB,)),
            dma((NB,)),
            dma((NB,)),
            dma((NB,)),
            dma((NB,)),
            dma((NB,)),
        ],
        compiler_params=pltpu.CompilerParams(
            collective_id=0, has_side_effects=True, vmem_limit_bytes=32 * 2**20
        ),
    )(
        *(
            pltpu.with_memory_space_constraint(array, pltpu.HBM)
            for array in (
                state,
                jnp.swapaxes(prior, 1, 2),
                value,
                error,
                place,
                height,
                jnp.transpose(blocks, (2, 1, 0)),
                jnp.transpose(counts),
                loc,
                mask,
            )
        )
    )
    analysis, post = pl.pallas_call(
        last_kernel,
        out_shape=(pltpu.HBM((LEVD, K, COLD), F32), pltpu.HBM((NB, OWN, K), F32)),
        in_specs=[vmem] * 6,
        out_specs=(hbm, hbm),
        scratch_shapes=[pltpu.VMEM((LEVD, K, COLD), F32), dma((LEVD,)), dma(())],
        compiler_params=pltpu.CompilerParams(vmem_limit_bytes=32 * 2**20),
    )(*carried)
    return analysis, jnp.swapaxes(post, 1, 2)


def solution(mesh):
    placed = (
        P("lev", None, "tile"),
        P(None, None, ("tile", "lev")),
        P(None, ("tile", "lev")),
        P(None, ("tile", "lev")),
        P(None, ("tile", "lev")),
        P(None, ("tile", "lev")),
        P(None, "tile", None),
        P(None, "tile"),
        P(None, None, "tile"),
        P(),
    )
    return jax.shard_map(
        per_device,
        mesh=mesh,
        in_specs=placed,
        out_specs=(P("lev", None, "tile"), P(None, None, ("tile", "lev"))),
        check_vma=False,
    )
```
